32 devices in a mesh: col: 4 (over z), row: 8 (over y, x, core).
Axes of the slice: x: 2, y: 2, z: 4, core: 2. Of those that a mesh axis runs over, the one named last changes fastest.
Arguments:
- inputs: bfloat16 [256, 8192], P('row', 'col'), may hold values from -6 to 6
- grad_out: bfloat16 [256, 8192], P('row', 'col'), may hold values from -6 to 6
- gate_pre: bfloat16 [256, 16384], P('col', 'row'), may hold values from -8 to 8
- up_pre: bfloat16 [256, 16384], P('col', 'row'), may hold values from -6 to 6
- gate_weight: bfloat16 [8192, 16384], P('col', 'row'), may hold values from -0.0625 to 0.0625
- up_weight: bfloat16 [8192, 16384], P('col', 'row'), may hold values from -0.0625 to 0.0625
- down_weight: bfloat16 [16384, 8192], P('row', 'col'), may hold values from -0.046875 to 0.046875
Outputs:
- input_grad: bfloat16 [256, 8192], P('row', 'col')
- gate_grad: bfloat16 [8192, 16384], P('col', 'row')
- up_grad: bfloat16 [8192, 16384], P('col', 'row')
- down_grad: bfloat16 [16384, 8192], P('row', 'col')
The draws below stay inside these ranges and needn't reach their ends.
All inputs are finite; a program needn't handle non-finite values.
Results may differ from the reference program's by a relative error of at most 0.0049.
Values may be sent and summed in bfloat16 or wider, within the bound.
No kernel may reach another device: no remote copies, remote signals or barrier semaphores. Data moves between devices by JAX's collectives and lax.ppermute only.
A program may use at most 128 MiB of HBM per device.

```python
import math
import jax
import jax.numpy as jnp

D = 8192
FF = 16384
TOKENS = 256


def raised(result, key, source, target, shards_of, factor):
    def block_of(axis_at):
        return (jnp.arange(result.shape[axis_at]) // (result.shape[axis_at] // shards_of)).reshape((-1,) + (1,) * (result.ndim - 1 - axis_at))

    near = jax.random.permutation(key, shards_of)[block_of(target)]
    far = (block_of(target) + shards_of // 2) % shards_of
    return jnp.where((block_of(source) == near) | (block_of(source) == far), factor * result, result)


def block_scale(rng, extent, shards, smallest, high):
    factor_of, own = 1.0, jax.random.fold_in(rng, 6)
    for dim, shards_of in shards:
        heights = jnp.exp(jax.random.uniform(jax.random.fold_in(own, dim), (shards_of,), jnp.float32, smallest / len(shards), high / len(shards)))
        factor_of = factor_of * jnp.repeat(heights, extent[dim] // shards_of).reshape([-1 if axis == dim else 1 for axis in range(len(extent))])
    return factor_of


def centred(stream_key, extent, width, bound, split=(), dtype=jnp.bfloat16):
    factor_of = block_scale(stream_key, extent, split, -0.22, 0.18) if split else 1.0
    result = jax.random.normal(stream_key, extent, jnp.float32) * width * factor_of
    return jnp.minimum(jnp.maximum(result, -bound), bound).astype(dtype)


def bell_draw_with(key, extent, spread, limit, split, heavy, dtype=jnp.bfloat16):
    entries = spread * jax.random.normal(key, extent, jnp.float32)
    if split:
        entries = entries * block_scale(key, extent, split, -0.22, 0.18)
    return jnp.clip(raised(entries, jax.random.fold_in(key, 3), *heavy), -limit, limit).astype(dtype)


def setup_inputs(seed: int = 0) -> dict:
    seeds = jax.random.split(jax.random.key(seed), 8)
    inputs = centred(seeds[0], (TOKENS, D), 1.0, 6.0, ((0, 8), (1, 4)))
    grad_out = bell_draw_with(seeds[1], (TOKENS, D), 1.0, 6.0, ((0, 8), (1, 4)), (1, 0, 8, 2.0))
    gate_pre = centred(seeds[2], (TOKENS, FF), 1.5, 8.0, ((0, 4), (1, 8)))
    up_pre = centred(seeds[3], (TOKENS, FF), 1.0, 6.0, ((0, 4), (1, 8)))
    gate_weight = centred(seeds[4], (D, FF), D ** -0.5, 0.0625, ((0, 4), (1, 8)))
    up_weight = centred(seeds[5], (D, FF), D ** -0.5, 0.0625, ((0, 4), (1, 8)))
    down_weight = centred(seeds[6], (FF, D), FF ** -0.5, 0.046875, ((0, 8), (1, 4)))
    return {"inputs": inputs, "grad_out": grad_out, "gate_pre": gate_pre, "up_pre": up_pre, "gate_weight": gate_weight, "up_weight": up_weight, "down_weight": down_weight}


def reference(inputs, grad_out, gate_pre, up_pre, gate_weight, up_weight, down_weight):
    hidden_grad = jnp.dot(grad_out, down_weight.T, preferred_element_type=jnp.float32)
    gate_val = gate_pre.astype(jnp.float32)
    up_val = up_pre.astype(jnp.float32)
    sigmoid_val = jax.nn.sigmoid(gate_val)
    silu_val = gate_val * sigmoid_val
    hidden = (silu_val * up_val).astype(jnp.bfloat16)
    up_term = (hidden_grad * silu_val).astype(jnp.bfloat16)
    gate_term = (hidden_grad * up_val * sigmoid_val * (1.0 + gate_val * (1.0 - sigmoid_val))).astype(jnp.bfloat16)
    grad_scale = 1.0 / math.sqrt(TOKENS)
    down_grad = (jnp.dot(hidden.T, grad_out, preferred_element_type=jnp.float32) * grad_scale).astype(jnp.bfloat16)
    gate_grad = (jnp.dot(inputs.T, gate_term, preferred_element_type=jnp.float32) * grad_scale).astype(jnp.bfloat16)
    up_grad = (jnp.dot(inputs.T, up_term, preferred_element_type=jnp.float32) * grad_scale).astype(jnp.bfloat16)
    input_grad = (jnp.dot(gate_term, gate_weight.T, preferred_element_type=jnp.float32) + jnp.dot(up_term, up_weight.T, preferred_element_type=jnp.float32)).astype(jnp.bfloat16)
    return (input_grad, gate_grad, up_grad, down_grad)
```

```python
import functools
import math

import jax
import jax.numpy as jnp
from jax import lax
from jax.experimental import pallas as pl
from jax.experimental.pallas import tpu as pltpu
from jax.sharding import PartitionSpec as P

F32, BF16 = jnp.float32, jnp.bfloat16
VMEM_LIMIT = 40 * 1024 * 1024
STRIPE = 256


def stripe(extent):
    return math.gcd(extent, STRIPE)


def whole(shape):
    return pl.BlockSpec(shape, lambda i, *_: (0,) * len(shape))


def params():
    return pltpu.CompilerParams(vmem_limit_bytes=VMEM_LIMIT, dimension_semantics=("arbitrary",))


def flip(count, mask):
    return [(i, i ^ mask) for i in range(count)]


def turn(count, shift):
    return [(i, (i + shift) % count) for i in range(count)]


def gather_row(own, n_row):
    pieces = [own] + [None] * (n_row - 1)
    for mask in range(2, n_row, 2):
        pieces[mask] = lax.ppermute(own, "row", flip(n_row, mask))
    for mask in range(0, n_row, 2):
        pieces[mask ^ 1] = lax.ppermute(pieces[mask], "row", flip(n_row, 1))
    return pieces


def relay_col(own, n_col):
    from_low, from_high = [own], [own]
    for step in range(1, n_col):
        up = [(i, i + 1) for i in range(step - 1, n_col - 1)]
        down = [(i, i - 1) for i in range(1, n_col - step + 1)]
        from_low.append(lax.ppermute(from_low[-1], "col", up))
        from_high.append(lax.ppermute(from_high[-1], "col", down))
    return from_low, from_high


def hidden_kernel(n_row, n_col, offsets, *refs):
    pieces, weight = refs[:n_row], refs[n_row]
    grad_all, own, sends = refs[n_row + 1], refs[n_row + 2], refs[n_row + 3 :]
    rows = pieces[0].shape[0]

    @pl.when(pl.program_id(0) == 0)
    def _():
        for x in range(n_row):
            grad_all[pl.ds(pl.multiple_of(offsets[x], rows), rows), :] = pieces[x][...]

    total = lax.dot_general(
        grad_all[...], weight[...], (((1,), (1,)), ((), ())), preferred_element_type=F32
    )
    part = own.shape[0]
    own[...] = total[:part]
    for j in range(1, n_col):
        sends[j - 1][...] = total[j * part : (j + 1) * part].astype(BF16)


def partial_hidden(pieces, weight, offsets, n_col):
    n_row = len(pieces)
    rows, width = pieces[0].shape
    units = weight.shape[0]
    tokens = rows * n_row
    part = tokens // n_col
    step = stripe(units)
    return pl.pallas_call(
        functools.partial(hidden_kernel, n_row, n_col),
        grid_spec=pltpu.PrefetchScalarGridSpec(
            num_scalar_prefetch=1,
            grid=(units // step,),
            in_specs=[whole((rows, width))] * n_row + [pl.BlockSpec((step, width), lambda i, *_: (i, 0))],
            out_specs=[whole((tokens, width))] + [pl.BlockSpec((part, step), lambda i, *_: (0, i))] * n_col,
        ),
        out_shape=[jax.ShapeDtypeStruct((tokens, width), BF16), jax.ShapeDtypeStruct((part, units), F32)]
        + [jax.ShapeDtypeStruct((part, units), BF16)] * (n_col - 1),
        compiler_params=params(),
        cost_estimate=pl.CostEstimate(
            flops=2 * tokens * width * units, bytes_accessed=2 * units * width, transcendentals=0
        ),
        name="partial_hidden",
    )(offsets, *pieces, weight)


def down_kernel(n_col, scale, place, *refs):
    gate, up, grad_all = refs[:3]
    from_low, from_high = refs[3 : 2 + n_col], refs[2 + n_col : 1 + 2 * n_col]
    down_grad, up_factor, gate_factor = refs[1 + 2 * n_col :]
    part = gate.shape[0]
    hidden = []
    for j in range(n_col):
        if j == 0:
            g, u = gate[...], up[...]
        else:
            low = place[0] >= j
            g = jnp.where(low, from_low[j - 1][0], from_high[n_col - j - 1][0])
            u = jnp.where(low, from_low[j - 1][1], from_high[n_col - j - 1][1])
        g, u = g.astype(F32), u.astype(F32)
        s = 1.0 / (1.0 + jnp.exp(-g))
        silu = g * s
        hidden.append((silu * u).astype(BF16))
        up_factor[j * part : (j + 1) * part, :] = silu
        gate_factor[j * part : (j + 1) * part, :] = u * s * (1.0 + g * (1.0 - s))
    product = lax.dot_general(
        jnp.concatenate(hidden, axis=0), grad_all[...], (((0,), (0,)), ((), ())), preferred_element_type=F32
    )
    down_grad[...] = (product * scale).astype(BF16)


def down_gradient(gate, up, grad_all, from_low, from_high, place, scale):
    n_col = len(from_low)
    part, units = gate.shape
    tokens, width = grad_all.shape
    step = stripe(units)
    flat = pl.BlockSpec((part, step), lambda i, *_: (0, i))
    pair = pl.BlockSpec((2, part, step), lambda i, *_: (0, 0, i))
    tall = pl.BlockSpec((tokens, step), lambda i, *_: (0, i))
    return pl.pallas_call(
        functools.partial(down_kernel, n_col, scale),
        grid_spec=pltpu.PrefetchScalarGridSpec(
            num_scalar_prefetch=1,
            grid=(units // step,),
            in_specs=[flat, flat, whole((tokens, width))] + [pair] * (2 * n_col - 2),
            out_specs=[pl.BlockSpec((step, width), lambda i, *_: (i, 0)), tall, tall],
        ),
        out_shape=[jax.ShapeDtypeStruct((units, width), BF16)] + [jax.ShapeDtypeStruct((tokens, units), F32)] * 2,
        compiler_params=params(),
        cost_estimate=pl.CostEstimate(
            flops=2 * tokens * width * units,
            bytes_accessed=2 * units * width + 12 * tokens * units,
            transcendentals=tokens * units,
        ),
        name="down_gradient",
    )(place, gate, up, grad_all, *from_low[1:], *from_high[1:])


def input_kernel(n_row, n_col, offsets, *refs):
    hidden_grad, refs = refs[:n_col], refs[n_col:]
    up_factor, gate_factor, gate_weight, up_weight, gate_term, up_term, own, other = refs
    part = hidden_grad[0].shape[0]
    rows = part * n_col // n_row

    @pl.when(pl.program_id(0) == 0)
    def _():
        for j in range(n_col):
            h = hidden_grad[j][...].astype(F32)
            at = slice(j * part, (j + 1) * part)
            terms = ((gate_term, (h * gate_factor[at, :]).astype(BF16)), (up_term, (h * up_factor[at, :]).astype(BF16)))
            for c in range(part // rows):
                to = pl.ds(pl.multiple_of(offsets[j * (part // rows) + c], rows), rows)
                for ref, term in terms:
                    ref[to, :] = term[c * rows : (c + 1) * rows]

    contract = (((1,), (1,)), ((), ()))
    total = lax.dot_general(gate_term[...], gate_weight[...], contract, preferred_element_type=F32)
    total += lax.dot_general(up_term[...], up_weight[...], contract, preferred_element_type=F32)
    half = own.shape[0]
    own[...] = total[:half]
    other[...] = total[half:].astype(BF16)


def partial_input(hidden_grad, up_factor, gate_factor, gate_weight, up_weight, offsets, n_row):
    n_col = len(hidden_grad)
    part, units = hidden_grad[0].shape
    tokens = part * n_col
    width = gate_weight.shape[0]
    step = stripe(width)
    weight = pl.BlockSpec((step, units), lambda i, *_: (i, 0))
    half = pl.BlockSpec((tokens // 2, step), lambda i, *_: (0, i))
    return pl.pallas_call(
        functools.partial(input_kernel, n_row, n_col),
        grid_spec=pltpu.PrefetchScalarGridSpec(
            num_scalar_prefetch=1,
            grid=(width // step,),
            in_specs=[whole((part, units))] * n_col + [whole((tokens, units))] * 2 + [weight, weight],
            out_specs=[whole((tokens, units))] * 2 + [half, half],
        ),
        out_shape=[jax.ShapeDtypeStruct((tokens, units), BF16)] * 2
        + [jax.ShapeDtypeStruct((tokens // 2, width), F32), jax.ShapeDtypeStruct((tokens // 2, width), BF16)],
        compiler_params=params(),
        cost_estimate=pl.CostEstimate(
            flops=4 * tokens * width * units, bytes_accessed=4 * units * width, transcendentals=0
        ),
        name="partial_input",
    )(offsets, *hidden_grad, up_factor, gate_factor, gate_weight, up_weight)


def weight_kernel(n_row, scale, *refs):
    pieces = refs[:n_row]
    gate_term, up_term, gate_grad, up_grad = refs[n_row:]
    order = list(range(0, n_row, 2)) + list(range(1, n_row, 2))
    left = jnp.concatenate([pieces[x][...] for x in order], axis=0)
    for term, out in ((gate_term, gate_grad), (up_term, up_grad)):
        product = lax.dot_general(left, term[...], (((0,), (0,)), ((), ())), preferred_element_type=F32)
        out[...] = (product * scale).astype(BF16)


def weight_gradients(pieces, gate_term, up_term, scale):
    n_row = len(pieces)
    rows, width = pieces[0].shape
    tokens, units = gate_term.shape
    step = stripe(width)
    out = pl.BlockSpec((step, units), lambda i: (i, 0))
    return pl.pallas_call(
        functools.partial(weight_kernel, n_row, scale),
        grid=(width // step,),
        in_specs=[pl.BlockSpec((rows, step), lambda i: (0, i))] * n_row + [whole((tokens, units))] * 2,
        out_specs=[out, out],
        out_shape=[jax.ShapeDtypeStruct((width, units), BF16)] * 2,
        compiler_params=params(),
        cost_estimate=pl.CostEstimate(
            flops=4 * tokens * width * units, bytes_accessed=4 * units * width, transcendentals=0
        ),
        name="weight_gradients",
    )(*pieces, gate_term, up_term)


def per_device(inputs, grad_out, gate_pre, up_pre, gate_weight, up_weight, down_weight):
    n_row, n_col = lax.axis_size("row"), lax.axis_size("col")
    row, col = lax.axis_index("row"), lax.axis_index("col")
    rows = grad_out.shape[0]
    tokens = rows * n_row
    share = n_row // n_col
    scale = 1.0 / math.sqrt(tokens)

    block = row ^ jnp.arange(n_row, dtype=jnp.int32)
    part_offsets = (jnp.mod(col - block // share, n_col) * share + block % share) * rows
    block = (jnp.mod(col - jnp.arange(n_col, dtype=jnp.int32), n_col)[:, None] * share + jnp.arange(share)).reshape(-1)
    seen = block ^ row
    block_offsets = ((seen % 2) * (n_row // 2) + seen // 2) * rows

    grad_pieces = gather_row(grad_out, n_row)
    from_low, from_high = relay_col(jnp.stack([gate_pre, up_pre]), n_col)
    grad_all, own, *sends = partial_hidden(grad_pieces, down_weight, part_offsets.astype(jnp.int32), n_col)
    for j, send in enumerate(sends, 1):
        own = own + lax.ppermute(send, "col", turn(n_col, -j)).astype(F32)
    own = own.astype(BF16)
    hidden_grad = [own] + [lax.ppermute(own, "col", turn(n_col, j)) for j in range(1, n_col)]

    down_grad, up_factor, gate_factor = down_gradient(
        gate_pre, up_pre, grad_all, from_low, from_high, col[None].astype(jnp.int32), scale
    )
    gate_term, up_term, mine, other = partial_input(
        hidden_grad, up_factor, gate_factor, gate_weight, up_weight, block_offsets.astype(jnp.int32), n_row
    )
    mine = mine + lax.ppermute(other, "row", flip(n_row, 1)).astype(F32)
    input_pieces = gather_row(inputs, n_row)
    input_grad = mine[:rows]
    for k in range(1, n_row // 2):
        away = mine[k * rows : (k + 1) * rows].astype(BF16)
        input_grad = input_grad + lax.ppermute(away, "row", flip(n_row, 2 * k)).astype(F32)
    gate_grad, up_grad = weight_gradients(input_pieces, gate_term, up_term, scale)
    return (input_grad.astype(BF16), gate_grad, up_grad, down_grad)


def solution(mesh):
    return jax.shard_map(
        per_device,
        mesh=mesh,
        in_specs=(
            P("row", "col"),
            P("row", "col"),
            P("col", "row"),
            P("col", "row"),
            P("col", "row"),
            P("col", "row"),
            P("row", "col"),
        ),
        out_specs=(P("row", "col"), P("col", "row"), P("col", "row"), P("row", "col")),
        check_vma=False,
    )
```

```python
import functools
import math

import jax
import jax.numpy as jnp
from jax import lax
from jax.experimental import pallas as pl
from jax.experimental.pallas import tpu as pltpu
from jax.sharding import PartitionSpec as P

F32, BF16 = jnp.float32, jnp.bfloat16
MIB = 1024 * 1024
STRIPE = 256


def stripe(extent):
    return math.gcd(extent, STRIPE)


def params(mib):
    return pltpu.CompilerParams(vmem_limit_bytes=mib * MIB)


def flip(count, mask):
    return [(i, i ^ mask) for i in range(count)]


def turn(count, shift):
    return [(i, (i + shift) % count) for i in range(count)]


def gather_row(own, n_row):
    mine = jnp.stack([own] + [lax.ppermute(own, "row", flip(n_row, mask)) for mask in range(2, n_row, 2)])
    return mine, lax.ppermute(mine, "row", flip(n_row, 1))


def relay_col(own, n_col):
    from_low, from_high = [own], [own]
    for step in range(1, n_col):
        up = [(i, i + 1) for i in range(step - 1, n_col - 1)]
        down = [(i, i - 1) for i in range(1, n_col - step + 1)]
        from_low.append(lax.ppermute(from_low[-1], "col", up))
        from_high.append(lax.ppermute(from_high[-1], "col", down))
    return from_low, from_high


def fetch_kernel(count, *refs):
    sources, targets, arrived = refs[:count], refs[-1 - count : -1], refs[-1]
    copies = []
    for k in range(count):
        rows = sources[k].shape[0] // arrived.shape[1]
        for i in range(arrived.shape[1]):
            at = pl.ds(i * rows, rows)
            copies.append(pltpu.make_async_copy(sources[k].at[at, :], targets[k].at[at, :], arrived.at[k, i]))
            copies[-1].start()
    for copy in copies:
        copy.wait()


def fetch(weights, after=()):
    size = sum(w.size * 2 for w in weights)
    return pl.pallas_call(
        functools.partial(fetch_kernel, len(weights)),
        in_specs=[IN_HBM] * len(weights) + [IN_ANY] * len(after),
        out_specs=[IN_VMEM] * len(weights),
        out_shape=[jax.ShapeDtypeStruct(w.shape, w.dtype) for w in weights],
        scratch_shapes=[pltpu.SemaphoreType.DMA((len(weights), 4))],
        compiler_params=params(1),
        cost_estimate=pl.CostEstimate(flops=0, bytes_accessed=size, transcendentals=0),
        name="fetch",
    )(*weights, *after)


def store(buffer, hbm, semaphores, i):
    rows = buffer.shape[0] // semaphores.shape[0]
    at = pl.ds(i * rows, rows)
    copy = pltpu.make_async_copy(buffer.at[at, :], hbm.at[at, :], semaphores.at[i])
    copy.start()
    return copy


IN_VMEM = pl.BlockSpec(memory_space=pltpu.VMEM)
IN_SMEM = pl.BlockSpec(memory_space=pltpu.SMEM)
IN_HBM = pl.BlockSpec(memory_space=pltpu.HBM)
IN_ANY = pl.BlockSpec(memory_space=pl.ANY)
NT = (((1,), (1,)), ((), ()))
TN = (((0,), (0,)), ((), ()))


def hidden_kernel(n_row, n_col, offsets, mine, theirs, weight, grad_all, own, *sends):
    rows, part = mine.shape[1], own.shape[0]
    for x in range(n_row):
        grad_all[pl.ds(pl.multiple_of(offsets[x], rows), rows), :] = (theirs if x % 2 else mine)[x // 2]
    step = stripe(weight.shape[0])
    for i in range(weight.shape[0] // step):
        at = slice(i * step, (i + 1) * step)
        total = lax.dot_general(grad_all[...], weight[at, :], NT, preferred_element_type=F32)
        own[:, at] = total[:part]
        for j in range(1, n_col):
            sends[j - 1][:, at] = total[j * part : (j + 1) * part].astype(BF16)


def partial_hidden(mine, theirs, weight, offsets, n_col):
    n_row, rows, width = 2 * mine.shape[0], mine.shape[1], mine.shape[2]
    units = weight.shape[0]
    tokens = rows * n_row
    part = tokens // n_col
    return pl.pallas_call(
        functools.partial(hidden_kernel, n_row, n_col),
        in_specs=[IN_SMEM] + [IN_VMEM] * 3,
        out_specs=[IN_VMEM] * (1 + n_col),
        out_shape=[jax.ShapeDtypeStruct((tokens, width), BF16), jax.ShapeDtypeStruct((part, units), F32)]
        + [jax.ShapeDtypeStruct((part, units), BF16)] * (n_col - 1),
        compiler_params=params(8),
        cost_estimate=pl.CostEstimate(
            flops=2 * tokens * width * units, bytes_accessed=2 * units * width, transcendentals=0
        ),
        name="partial_hidden",
    )(offsets, mine, theirs, weight)


def down_kernel(n_col, scale, place, *refs):
    gate, up, grad_all, mine, theirs = refs[:5]
    from_low, from_high = refs[5 : 4 + n_col], refs[4 + n_col : 3 + 2 * n_col]
    down_grad, up_factor, gate_factor, input_all, buffer, left = refs[3 + 2 * n_col :]
    blocks, rows = mine.shape[:2]
    for k in range(blocks):
        input_all[k * rows : (k + 1) * rows, :] = mine[k]
        input_all[(blocks + k) * rows : (blocks + k + 1) * rows, :] = theirs[k]
    part, units = gate.shape
    step = units // left.shape[0]
    copies = []
    for i in range(left.shape[0]):
        at = slice(i * step, (i + 1) * step)
        hidden = []
        for j in range(n_col):
            if j == 0:
                g, u = gate[:, at], up[:, at]
            else:
                low = place[0] >= j
                g = jnp.where(low, from_low[j - 1][0, :, at], from_high[n_col - j - 1][0, :, at])
                u = jnp.where(low, from_low[j - 1][1, :, at], from_high[n_col - j - 1][1, :, at])
            g, u = g.astype(F32), u.astype(F32)
            s = 1.0 / (1.0 + jnp.exp(-g))
            silu = g * s
            hidden.append((silu * u).astype(BF16))
            up_factor[j * part : (j + 1) * part, at] = silu
            gate_factor[j * part : (j + 1) * part, at] = u * s * (1.0 + g * (1.0 - s))
        product = lax.dot_general(
            jnp.concatenate(hidden, axis=0), grad_all[...], TN, preferred_element_type=F32
        )
        buffer[at, :] = (product * scale).astype(BF16)
        copies.append(store(buffer, down_grad, left, i))
    for copy in copies:
        copy.wait()


def down_gradient(gate, up, grad_all, mine, theirs, from_low, from_high, place, scale):
    n_col = len(from_low)
    part, units = gate.shape
    tokens, width = grad_all.shape
    return pl.pallas_call(
        functools.partial(down_kernel, n_col, scale),
        in_specs=[IN_SMEM] + [IN_VMEM] * (2 * n_col + 3),
        out_specs=[IN_HBM] + [IN_VMEM] * 3,
        out_shape=[jax.ShapeDtypeStruct((units, width), BF16)]
        + [jax.ShapeDtypeStruct((tokens, units), F32)] * 2
        + [jax.ShapeDtypeStruct((tokens, width), BF16)],
        scratch_shapes=[pltpu.VMEM((units, width), BF16), pltpu.SemaphoreType.DMA((units // stripe(units),))],
        compiler_params=params(16),
        cost_estimate=pl.CostEstimate(
            flops=2 * tokens * width * units,
            bytes_accessed=2 * units * width + 12 * tokens * units,
            transcendentals=tokens * units,
        ),
        name="down_gradient",
    )(place, gate, up, grad_all, mine, theirs, *from_low[1:], *from_high[1:])


def input_kernel(n_row, n_col, offsets, *refs):
    hidden_grad, refs = refs[:n_col], refs[n_col:]
    up_factor, gate_factor, gate_weight, up_weight, gate_term, up_term, own, other = refs
    part = hidden_grad[0].shape[0]
    rows = part * n_col // n_row
    half = own.shape[0]
    for j in range(n_col):
        h = hidden_grad[j][...].astype(F32)
        at = slice(j * part, (j + 1) * part)
        terms = ((gate_term, (h * gate_factor[at, :]).astype(BF16)), (up_term, (h * up_factor[at, :]).astype(BF16)))
        for c in range(part // rows):
            to = pl.ds(pl.multiple_of(offsets[j * (part // rows) + c], rows), rows)
            for ref, term in terms:
                ref[to, :] = term[c * rows : (c + 1) * rows]
    step = stripe(own.shape[1])
    for i in range(own.shape[1] // step):
        at = slice(i * step, (i + 1) * step)
        total = lax.dot_general(gate_term[...], gate_weight[at, :], NT, preferred_element_type=F32)
        total += lax.dot_general(up_term[...], up_weight[at, :], NT, preferred_element_type=F32)
        own[:, at] = total[:half]
        other[:, at] = total[half:]


def partial_input(hidden_grad, up_factor, gate_factor, gate_weight, up_weight, offsets, n_row):
    n_col = len(hidden_grad)
    part, units = hidden_grad[0].shape
    tokens = part * n_col
    width = gate_weight.shape[0]
    return pl.pallas_call(
        functools.partial(input_kernel, n_row, n_col),
        in_specs=[IN_SMEM] + [IN_VMEM] * (n_col + 4),
        out_specs=[IN_VMEM] * 4,
        out_shape=[jax.ShapeDtypeStruct((tokens, units), BF16)] * 2
        + [jax.ShapeDtypeStruct((tokens // 2, width), F32)] * 2,
        compiler_params=params(8),
        cost_estimate=pl.CostEstimate(
            flops=4 * tokens * width * units, bytes_accessed=4 * units * width, transcendentals=0
        ),
        name="partial_input",
    )(offsets, *hidden_grad, up_factor, gate_factor, gate_weight, up_weight)


def weight_kernel(scale, input_all, gate_term, up_term, gate_grad, up_grad, buffers, left):
    step = buffers.shape[1] // left.shape[1]
    copies = []
    for i in range(left.shape[1]):
        at = slice(i * step, (i + 1) * step)
        for k, (term, out) in enumerate(((gate_term, gate_grad), (up_term, up_grad))):
            product = lax.dot_general(input_all[:, at], term[...], TN, preferred_element_type=F32)
            buffers[k, at, :] = (product * scale).astype(BF16)
            copies.append(store(buffers.at[k], out, left.at[k], i))
    for copy in copies:
        copy.wait()


def weight_gradients(input_all, gate_term, up_term, scale):
    tokens, width = input_all.shape
    units = gate_term.shape[1]
    return pl.pallas_call(
        functools.partial(weight_kernel, scale),
        in_specs=[IN_VMEM] * 3,
        out_specs=[IN_HBM] * 2,
        out_shape=[jax.ShapeDtypeStruct((width, units), BF16)] * 2,
        scratch_shapes=[
            pltpu.VMEM((2, width, units), BF16),
            pltpu.SemaphoreType.DMA((2, width // stripe(width))),
        ],
        compiler_params=params(24),
        cost_estimate=pl.CostEstimate(
            flops=4 * tokens * width * units, bytes_accessed=4 * units * width, transcendentals=0
        ),
        name="weight_gradients",
    )(input_all, gate_term, up_term)


def per_device(inputs, grad_out, gate_pre, up_pre, gate_weight, up_weight, down_weight):
    n_row, n_col = lax.axis_size("row"), lax.axis_size("col")
    row, col = lax.axis_index("row"), lax.axis_index("col")
    rows = grad_out.shape[0]
    tokens = rows * n_row
    share = n_row // n_col
    scale = 1.0 / math.sqrt(tokens)

    block = row ^ jnp.arange(n_row, dtype=jnp.int32)
    part_offsets = (jnp.mod(col - block // share, n_col) * share + block % share) * rows
    block = (jnp.mod(col - jnp.arange(n_col, dtype=jnp.int32), n_col)[:, None] * share + jnp.arange(share)).reshape(-1)
    seen = block ^ row
    block_offsets = ((seen % 2) * (n_row // 2) + seen // 2) * rows

    (fetched,) = fetch([down_weight])
    grad_mine, grad_theirs = gather_row(grad_out, n_row)
    from_low, from_high = relay_col(jnp.stack([gate_pre, up_pre]), n_col)
    grad_all, own, *sends = partial_hidden(
        grad_mine, grad_theirs, fetched, part_offsets.astype(jnp.int32), n_col
    )
    for j, send in enumerate(sends, 1):
        own = own + lax.ppermute(send, "col", turn(n_col, -j)).astype(F32)
    own = own.astype(BF16)
    hidden_grad = [own] + [lax.ppermute(own, "col", turn(n_col, j)) for j in range(1, n_col)]

    input_mine, input_theirs = gather_row(inputs, n_row)
    down_grad, up_factor, gate_factor, input_all = down_gradient(
        gate_pre, up_pre, grad_all, input_mine, input_theirs, from_low, from_high, col[None].astype(jnp.int32), scale
    )
    gate_fetched, up_fetched = fetch([gate_weight, up_weight], after=[own])
    gate_term, up_term, mine, other = partial_input(
        hidden_grad, up_factor, gate_factor, gate_fetched, up_fetched, block_offsets.astype(jnp.int32), n_row
    )
    mine = mine + lax.ppermute(other, "row", flip(n_row, 1))
    input_grad = mine[:rows]
    for k in range(1, n_row // 2):
        away = mine[k * rows : (k + 1) * rows].astype(BF16)
        input_grad = input_grad + lax.ppermute(away, "row", flip(n_row, 2 * k)).astype(F32)
    gate_grad, up_grad = weight_gradients(input_all, gate_term, up_term, scale)
    return (input_grad.astype(BF16), gate_grad, up_grad, down_grad)


def solution(mesh):
    return jax.shard_map(
        per_device,
        mesh=mesh,
        in_specs=(
            P("row", "col"),
            P("row", "col"),
            P("col", "row"),
            P("col", "row"),
            P("col", "row"),
            P("col", "row"),
            P("row", "col"),
        ),
        out_specs=(P("row", "col"), P("col", "row"), P("col", "row"), P("row", "col")),
        check_vma=False,
    )
```

```python
import functools
import math

import jax
import jax.numpy as jnp
from jax import lax
from jax.experimental import pallas as pl
from jax.experimental.pallas import tpu as pltpu
from jax.sharding import PartitionSpec as P

F32, BF16 = jnp.float32, jnp.bfloat16
MIB = 1024 * 1024
STRIPE = 256


def pinned(*arrays):
    return [pltpu.with_memory_space_constraint(array, pltpu.HBM) for array in arrays]


def stripe(extent):
    return math.gcd(extent, STRIPE)


def params(mib):
    return pltpu.CompilerParams(vmem_limit_bytes=mib * MIB)


def flip(count, mask):
    return [(i, i ^ mask) for i in range(count)]


def swap(block, axis, mask):
    return lax.ppermute(block, axis, flip(lax.axis_size(axis), mask))


def after(later, earlier):
    return lax.optimization_barrier((later, earlier))


def spread_col(own, token, n_col):
    parts = {0: own}
    mask = n_col // 2
    while mask:
        for p in list(parts):
            block = parts[p]
            if p:
                block, token = after(block, token)
            parts[p | mask] = swap(block, "col", mask)
        mask //= 2
    return [parts[p] for p in range(n_col)]


def reduce_halves(parts, sends, n_col):
    parts, arrived, onward = {**parts, **sends}, [], None
    mask = 1
    while mask < n_col:
        blocks = {p: swap(parts.pop(p).astype(BF16), "col", mask) for p in list(parts) if p & mask}
        arrived.append(blocks.pop(mask))
        for p, block in blocks.items():
            onward = parts[p ^ mask] = parts[p ^ mask] + block.astype(F32)
        mask *= 2
    return arrived, onward


def reduce_line(parts, sends, col):
    right = lax.ppermute(sends[2], "col", [(0, 1), (1, 2)]).astype(F32)
    left = lax.ppermute(sends[2], "col", [(3, 2), (2, 1)]).astype(F32)
    over = lax.ppermute(sends[3], "col", [(0, 2), (3, 1)]).astype(F32)
    right = right + jnp.where(col == 1, parts[3], parts[1]) + jnp.where(col == 2, over, 0.0)
    left = left + jnp.where(col == 2, parts[3], parts[1]) + jnp.where(col == 1, over, 0.0)
    right, left = right.astype(BF16), left.astype(BF16)
    arrived = [
        lax.ppermute(right, "col", [(0, 1), (1, 2), (2, 3)]),
        lax.ppermute(left, "col", [(3, 2), (2, 1), (1, 0)]),
    ]
    return arrived, right


def relay_col(low, high, n_col, step):
    up = [(i, i + 1) for i in range(step - 1, n_col - 1)]
    down = [(i, i - 1) for i in range(1, n_col - step + 1)]
    return lax.ppermute(low, "col", up), lax.ppermute(high, "col", down)


def spread_row(own, n_row):
    mine = own[None]
    mask = 2
    while mask < n_row:
        mine = jnp.concatenate([mine, swap(mine, "row", mask)])
        mask *= 2
    return mine


def fetch_kernel(count, *refs):
    sources, (*targets, token, arrived) = refs[:count], refs[-2 - count :]
    token[...] = jnp.zeros_like(token)
    copies = []
    for k in range(count):
        rows = sources[k].shape[0] // arrived.shape[1]
        for i in range(arrived.shape[1]):
            at = pl.ds(i * rows, rows)
            copies.append(pltpu.make_async_copy(sources[k].at[at, :], targets[k].at[at, :], arrived.at[k, i]))
            copies[-1].start()
    for copy in copies:
        copy.wait()


def fetch(weights, behind=()):
    size = sum(w.size * 2 for w in weights)
    return pl.pallas_call(
        functools.partial(fetch_kernel, len(weights)),
        in_specs=[IN_HBM] * len(weights) + [IN_ANY] * len(behind),
        out_specs=[IN_VMEM] * (len(weights) + 1),
        out_shape=[jax.ShapeDtypeStruct(w.shape, w.dtype) for w in weights] + [jax.ShapeDtypeStruct((8, 128), F32)],
        scratch_shapes=[pltpu.SemaphoreType.DMA((len(weights), 4))],
        compiler_params=params(1),
        cost_estimate=pl.CostEstimate(flops=0, bytes_accessed=1024, transcendentals=0),
        name="fetch",
    )(*pinned(*weights), *behind)


def store(buffer, hbm, semaphores, i):
    rows = buffer.shape[0] // semaphores.shape[0]
    at = pl.ds(i * rows, rows)
    copy = pltpu.make_async_copy(buffer.at[at, :], hbm.at[at, :], semaphores.at[i])
    copy.start()
    return copy


IN_VMEM = pl.BlockSpec(memory_space=pltpu.VMEM)
IN_SMEM = pl.BlockSpec(memory_space=pltpu.SMEM)
IN_HBM = pl.BlockSpec(memory_space=pltpu.HBM)
IN_ANY = pl.BlockSpec(memory_space=pl.ANY)
NT = (((1,), (1,)), ((), ()))
TN = (((0,), (0,)), ((), ()))


def stack_kernel(count, *refs):
    for k in range(count):
        refs[-1][k] = refs[k][...]


def stacked(blocks, behind):
    return pl.pallas_call(
        functools.partial(stack_kernel, len(blocks)),
        in_specs=[IN_VMEM] * len(blocks) + [IN_ANY] * len(behind),
        out_specs=IN_VMEM,
        out_shape=jax.ShapeDtypeStruct((len(blocks),) + blocks[0].shape, blocks[0].dtype),
        compiler_params=params(2),
        name="stacked",
    )(*blocks, *behind)


def hidden_kernel(n_row, n_col, kept, early, offsets, mine, theirs, weight, *refs):
    grad_all, token, *parts = refs[-2 - len(kept) - len(early) :]
    token[...] = jnp.zeros_like(token)
    rows, part = mine.shape[1], parts[0].shape[0]
    kinds = [(p, F32) for p in kept] + [(p, BF16) for p in early]
    for x in range(n_row):
        grad_all[pl.ds(pl.multiple_of(offsets[x], rows), rows), :] = (theirs if x % 2 else mine)[x // 2]
    step = stripe(weight.shape[0])
    for i in range(weight.shape[0] // step):
        at = slice(i * step, (i + 1) * step)
        total = lax.dot_general(grad_all[...], weight[at, :], NT, preferred_element_type=F32)
        for ref, (p, kind) in zip(parts, kinds):
            ref[:, at] = total[p * part : (p + 1) * part].astype(kind)


def partial_hidden(mine, theirs, weight, behind, offsets, n_col, kept, early):
    n_row, rows, width = 2 * mine.shape[0], mine.shape[1], mine.shape[2]
    units = weight.shape[0]
    tokens = rows * n_row
    part = tokens // n_col
    grad_all, token, *parts = pl.pallas_call(
        functools.partial(hidden_kernel, n_row, n_col, kept, early),
        in_specs=[IN_SMEM] + [IN_VMEM] * 3 + [IN_HBM] * len(behind),
        out_specs=[IN_VMEM] * (2 + len(kept) + len(early)),
        out_shape=[jax.ShapeDtypeStruct((tokens, width), BF16), jax.ShapeDtypeStruct((8, 128), F32)]
        + [jax.ShapeDtypeStruct((part, units), F32)] * len(kept)
        + [jax.ShapeDtypeStruct((part, units), BF16)] * len(early),
        compiler_params=params(2),
        cost_estimate=pl.CostEstimate(
            flops=2 * tokens * width * units, bytes_accessed=2 * units * width, transcendentals=0
        ),
        name="partial_hidden",
    )(offsets, mine, theirs, weight, *pinned(*behind))
    return grad_all, token, dict(zip(kept, parts)), dict(zip(early, parts[len(kept) :]))


def sum_kernel(count, *refs):
    total = refs[0][...]
    for ref in refs[1:count]:
        total = total + ref[...].astype(F32)
    refs[-1][...] = total.astype(BF16)


def summed(own, arrived, behind):
    return pl.pallas_call(
        functools.partial(sum_kernel, 1 + len(arrived)),
        in_specs=[IN_VMEM] * (1 + len(arrived)) + [IN_ANY] * len(behind),
        out_specs=IN_VMEM,
        out_shape=jax.ShapeDtypeStruct(own.shape, BF16),
        compiler_params=params(2),
        cost_estimate=pl.CostEstimate(flops=own.size, bytes_accessed=8 * own.size, transcendentals=0),
        name="summed",
    )(own, *arrived, *behind)


def pick(from_low, from_high, p, col, which, at):
    n_col = len(from_low)
    value, known = from_low[0][which, :, at], set()
    for c in range(n_col):
        below, distance = (c ^ p) < c, abs((c ^ p) - c)
        if p and (below, distance) not in known:
            known.add((below, distance))
            block = (from_low if below else from_high)[distance][which, :, at]
            match = jnp.logical_and(((col ^ p) < col) == below, jnp.abs((col ^ p) - col) == distance)
            value = block if len(known) == 1 else jnp.where(match, block, value)
    return value.astype(F32)


def down_kernel(n_col, scale, place, *refs):
    moved, grad_all = refs[: 2 * n_col - 1], refs[2 * n_col - 1]
    down_grad, up_factor, gate_factor, saved, arrived, buffer, left = refs[-7:]
    loads = [pltpu.make_async_copy(block, saved.at[k], arrived.at[k]) for k, block in enumerate(moved)]
    for copy in loads:
        copy.start()
    for copy in loads:
        copy.wait()
    blocks = [saved.at[k] for k in range(len(moved))]
    from_low, from_high = blocks[:n_col], blocks[:1] + blocks[n_col:]
    _, part, units = from_low[0].shape
    col = place[0]
    step = units // left.shape[0]
    copies = []
    for i in range(left.shape[0]):
        at = slice(i * step, (i + 1) * step)
        hidden = []
        for p in range(n_col):
            g, u = (pick(from_low, from_high, p, col, which, at) for which in range(2))
            s = 1.0 / (1.0 + jnp.exp(-g))
            silu = g * s
            hidden.append((silu * u).astype(BF16))
            up_factor[p * part : (p + 1) * part, at] = silu
            gate_factor[p * part : (p + 1) * part, at] = u * s * (1.0 + g * (1.0 - s))
        product = lax.dot_general(
            jnp.concatenate(hidden, axis=0), grad_all[...], TN, preferred_element_type=F32
        )
        buffer[at, :] = (product * scale).astype(BF16)
        copies.append(store(buffer, down_grad, left, i))
    for copy in copies:
        copy.wait()


def down_gradient(from_low, from_high, grad_all, behind, place, scale):
    n_col = len(from_low)
    units = from_low[0].shape[2]
    tokens, width = grad_all.shape
    return pl.pallas_call(
        functools.partial(down_kernel, n_col, scale),
        in_specs=[IN_SMEM] + [IN_HBM] * (2 * n_col - 1) + [IN_VMEM] + [IN_ANY] * len(behind),
        out_specs=[IN_HBM] + [IN_VMEM] * 2,
        out_shape=[jax.ShapeDtypeStruct((units, width), BF16)] + [jax.ShapeDtypeStruct((tokens, units), F32)] * 2,
        scratch_shapes=[
            pltpu.VMEM((2 * n_col - 1,) + from_low[0].shape, BF16),
            pltpu.SemaphoreType.DMA((2 * n_col - 1,)),
            pltpu.VMEM((units, width), BF16),
            pltpu.SemaphoreType.DMA((units // stripe(units),)),
        ],
        compiler_params=params(14),
        cost_estimate=pl.CostEstimate(
            flops=1 * 2 * tokens * width * units,
            bytes_accessed=2 * units * width + 12 * tokens * units,
            transcendentals=tokens * units,
        ),
        name="down_gradient",
    )(place, *pinned(*from_low, *from_high[1:]), grad_all, *behind)


def input_kernel(n_row, n_col, offsets, *refs):
    hidden_grad, refs = refs[:n_col], refs[n_col:]
    up_factor, gate_factor, gate_weight, up_weight, _, gate_term, up_term, own, other, token = refs
    token[...] = jnp.zeros_like(token)
    part = hidden_grad[0].shape[0]
    rows = part * n_col // n_row
    half = own.shape[0]
    for j in range(n_col):
        h = hidden_grad[j][...].astype(F32)
        at = slice(j * part, (j + 1) * part)
        terms = ((gate_term, (h * gate_factor[at, :]).astype(BF16)), (up_term, (h * up_factor[at, :]).astype(BF16)))
        for c in range(part // rows):
            to = pl.ds(pl.multiple_of(offsets[j * (part // rows) + c], rows), rows)
            for ref, term in terms:
                ref[to, :] = term[c * rows : (c + 1) * rows]
    step = stripe(own.shape[1])
    for i in range(own.shape[1] // step):
        at = slice(i * step, (i + 1) * step)
        total = lax.dot_general(gate_term[...], gate_weight[at, :], NT, preferred_element_type=F32)
        total += lax.dot_general(up_term[...], up_weight[at, :], NT, preferred_element_type=F32)
        own[:, at] = total[:half]
        other[:, at] = total[half:]


def partial_input(hidden_grad, up_factor, gate_factor, gate_weight, up_weight, behind, offsets, n_row):
    n_col = len(hidden_grad)
    part, units = hidden_grad[0].shape
    tokens = part * n_col
    width = gate_weight.shape[0]
    return pl.pallas_call(
        functools.partial(input_kernel, n_row, n_col),
        in_specs=[IN_SMEM] + [IN_VMEM] * (n_col + 4) + [IN_ANY],
        out_specs=[IN_VMEM] * 5,
        out_shape=[jax.ShapeDtypeStruct((tokens, units), BF16)] * 2
        + [jax.ShapeDtypeStruct((tokens // 2, width), F32)] * 2
        + [jax.ShapeDtypeStruct((8, 128), F32)],
        compiler_params=params(2),
        cost_estimate=pl.CostEstimate(
            flops=4 * tokens * width * units, bytes_accessed=4 * units * width, transcendentals=0
        ),
        name="partial_input",
    )(offsets, *hidden_grad, up_factor, gate_factor, gate_weight, up_weight, behind)


def weight_kernel(scale, mine, theirs, gate_term, up_term, _, gate_grad, up_grad, buffers, left):
    blocks = mine.shape[0]
    step = buffers.shape[1] // left.shape[1]
    copies = []
    for i in range(left.shape[1]):
        at = slice(i * step, (i + 1) * step)
        left_side = jnp.concatenate([ref[k, :, at] for ref in (mine, theirs) for k in range(blocks)], axis=0)
        for k, (term, out) in enumerate(((gate_term, gate_grad), (up_term, up_grad))):
            product = lax.dot_general(left_side, term[...], TN, preferred_element_type=F32)
            buffers[k, at, :] = (product * scale).astype(BF16)
            copies.append(store(buffers.at[k], out, left.at[k], i))
    for copy in copies:
        copy.wait()


def weight_gradients(mine, theirs, gate_term, up_term, behind, scale):
    width = mine.shape[2]
    tokens, units = gate_term.shape
    return pl.pallas_call(
        functools.partial(weight_kernel, scale),
        in_specs=[IN_VMEM] * 4 + [IN_ANY],
        out_specs=[IN_HBM] * 2,
        out_shape=[jax.ShapeDtypeStruct((width, units), BF16)] * 2,
        scratch_shapes=[
            pltpu.VMEM((2, width, units), BF16),
            pltpu.SemaphoreType.DMA((2, width // stripe(width))),
        ],
        compiler_params=params(18),
        cost_estimate=pl.CostEstimate(
            flops=4 * tokens * width * units, bytes_accessed=4 * units * width, transcendentals=0
        ),
        name="weight_gradients",
    )(mine, theirs, gate_term, up_term, behind)


def per_device(inputs, grad_out, gate_pre, up_pre, gate_weight, up_weight, down_weight):
    n_row, n_col = lax.axis_size("row"), lax.axis_size("col")
    row, col = lax.axis_index("row"), lax.axis_index("col")
    rows = grad_out.shape[0]
    tokens = rows * n_row
    share = n_row // n_col
    scale = 1.0 / math.sqrt(tokens)

    block = row ^ jnp.arange(n_row, dtype=jnp.int32)
    to_parts = (((block // share) ^ col) * share + block % share) * rows
    part = col ^ jnp.arange(n_col, dtype=jnp.int32)
    seen = (part[:, None] * share + jnp.arange(share, dtype=jnp.int32)).reshape(-1) ^ row
    to_blocks = ((seen % 2) * (n_row // 2) + seen // 2) * rows

    near = [swap(grad_out, "row", mask) for mask in range(2, n_row, 2)]
    saved = jnp.stack([gate_pre, up_pre])
    low, high = relay_col(saved, saved, n_col, 1)
    from_low, from_high = [saved, low], [saved, high]
    grad_mine = stacked([grad_out] + near, [])
    fetched, _ = fetch([down_weight], [grad_mine])
    grad_theirs = swap(grad_mine, "row", 1)
    kept, early = ((0, 1, 3), (2, 3)) if n_col == 4 else (tuple(range(0, n_col, 2)), tuple(range(1, n_col, 2)))
    grad_all, token, parts, sends = partial_hidden(
        grad_mine, grad_theirs, fetched, [from_low[1], from_high[1]], to_parts.astype(jnp.int32), n_col, kept, early
    )

    (low, high), token = after((low, high), token)
    for step in range(2, n_col):
        low, high = relay_col(low, high, n_col, step)
        from_low.append(low)
        from_high.append(high)
    if n_col == 4:
        arrived, onward = reduce_line(parts, sends, col)
    else:
        arrived, onward = reduce_halves(parts, sends, n_col)
    (inputs, onward), token = after((inputs, onward[:8, :128]), token)
    input_mine = spread_row(inputs, n_row)
    own = summed(parts[0], arrived, [token, onward])
    gate_fetched, up_fetched, token = fetch([gate_weight, up_weight], [own])
    hidden_grad = spread_col(own, token, n_col)

    down_grad, up_factor, gate_factor = down_gradient(
        from_low, from_high, grad_all, [hidden_grad[n_col // 2]], col[None].astype(jnp.int32), scale
    )
    gate_term, up_term, mine, other, token = partial_input(
        hidden_grad, up_factor, gate_factor, gate_fetched, up_fetched, input_mine, to_blocks.astype(jnp.int32), n_row
    )

    mine = mine + swap(other, "row", 1)
    input_grad = mine[:rows]
    for k in range(1, n_row // 2):
        away = mine[k * rows : (k + 1) * rows].astype(BF16)
        input_grad = input_grad + swap(away, "row", 2 * k).astype(F32)
    input_mine, token = after(input_mine, token)
    input_theirs = swap(input_mine, "row", 1)
    gate_grad, up_grad = weight_gradients(input_mine, input_theirs, gate_term, up_term, token, scale)
    return (input_grad.astype(BF16), gate_grad, up_grad, down_grad)


def solution(mesh):
    return jax.shard_map(
        per_device,
        mesh=mesh,
        in_specs=(
            P("row", "col"),
            P("row", "col"),
            P("col", "row"),
            P("col", "row"),
            P("col", "row"),
            P("col", "row"),
            P("row", "col"),
        ),
        out_specs=(P("row", "col"), P("col", "row"), P("col", "row"), P("row", "col")),
        check_vma=False,
    )
```

```python
import functools
import math

import jax
import jax.numpy as jnp
from jax import lax
from jax.experimental import pallas as pl
from jax.experimental.pallas import tpu as pltpu
from jax.sharding import PartitionSpec as P

F32, BF16 = jnp.float32, jnp.bfloat16
MIB = 1024 * 1024
STRIPE = 256


def pinned(*arrays):
    return [pltpu.with_memory_space_constraint(array, pltpu.HBM) for array in arrays]


def stripe(extent):
    return math.gcd(extent, STRIPE)


def params(mib):
    return pltpu.CompilerParams(vmem_limit_bytes=mib * MIB)


def flip(count, mask):
    return [(i, i ^ mask) for i in range(count)]


def swap(block, axis, mask):
    return lax.ppermute(block, axis, flip(lax.axis_size(axis), mask))


def after(later, earlier):
    return lax.optimization_barrier((later, earlier))


def spread_col(own, token, n_col):
    parts = {0: own}
    mask = n_col // 2
    while mask:
        for p in list(parts):
            block = parts[p]
            if p:
                block, token = after(block, token)
            parts[p | mask] = swap(block, "col", mask)
        mask //= 2
    return [parts[p] for p in range(n_col)]


def reduce_halves(parts, sends, n_col):
    parts, arrived, onward = {**parts, **sends}, [], None
    mask = 1
    while mask < n_col:
        blocks = {p: swap(parts.pop(p).astype(BF16), "col", mask) for p in list(parts) if p & mask}
        arrived.append(blocks.pop(mask))
        for p, block in blocks.items():
            onward = parts[p ^ mask] = parts[p ^ mask] + block.astype(F32)
        mask *= 2
    return arrived, onward


def reduce_line(parts, sends, col):
    right = lax.ppermute(sends[2], "col", [(0, 1), (1, 2)]).astype(F32)
    left = lax.ppermute(sends[2], "col", [(3, 2), (2, 1)]).astype(F32)
    came_over = lax.ppermute(sends[3], "col", [(0, 2), (3, 1)])
    over = came_over.astype(F32)
    right = right + jnp.where(col == 1, parts[3], parts[1]) + jnp.where(col == 2, over, 0.0)
    left = left + jnp.where(col == 2, parts[3], parts[1]) + jnp.where(col == 1, over, 0.0)
    right, left = right.astype(BF16), left.astype(BF16)
    arrived = [
        lax.ppermute(right, "col", [(0, 1), (1, 2), (2, 3)]),
        lax.ppermute(left, "col", [(3, 2), (2, 1), (1, 0)]),
    ]
    return arrived, came_over


def relay_col(low, high, n_col, step):
    up = [(i, i + 1) for i in range(step - 1, n_col - 1)]
    down = [(i, i - 1) for i in range(1, n_col - step + 1)]
    return lax.ppermute(low, "col", up), lax.ppermute(high, "col", down)


def spread_row(own, n_row):
    mine = own[None]
    mask = 2
    while mask < n_row:
        mine = jnp.concatenate([mine, swap(mine, "row", mask)])
        mask *= 2
    return mine


def fetch_kernel(count, *refs):
    sources, (*targets, token, arrived) = refs[:count], refs[-2 - count :]
    token[...] = jnp.zeros_like(token)
    copies = []
    for k in range(count):
        rows = sources[k].shape[0] // arrived.shape[1]
        for i in range(arrived.shape[1]):
            at = pl.ds(i * rows, rows)
            copies.append(pltpu.make_async_copy(sources[k].at[at, :], targets[k].at[at, :], arrived.at[k, i]))
            copies[-1].start()
    for copy in copies:
        copy.wait()


def fetch(weights, behind=()):
    size = sum(w.size * 2 for w in weights)
    return pl.pallas_call(
        functools.partial(fetch_kernel, len(weights)),
        in_specs=[IN_HBM] * len(weights) + [IN_ANY] * len(behind),
        out_specs=[IN_VMEM] * (len(weights) + 1),
        out_shape=[jax.ShapeDtypeStruct(w.shape, w.dtype) for w in weights] + [jax.ShapeDtypeStruct((8, 128), F32)],
        scratch_shapes=[pltpu.SemaphoreType.DMA((len(weights), 4))],
        compiler_params=params(1),
        cost_estimate=pl.CostEstimate(flops=0, bytes_accessed=1024, transcendentals=0),
        name="fetch",
    )(*pinned(*weights), *behind)


def store(buffer, hbm, semaphores, i):
    rows = buffer.shape[0] // semaphores.shape[0]
    at = pl.ds(i * rows, rows)
    copy = pltpu.make_async_copy(buffer.at[at, :], hbm.at[at, :], semaphores.at[i])
    copy.start()
    return copy


IN_VMEM = pl.BlockSpec(memory_space=pltpu.VMEM)
IN_SMEM = pl.BlockSpec(memory_space=pltpu.SMEM)
IN_HBM = pl.BlockSpec(memory_space=pltpu.HBM)
IN_ANY = pl.BlockSpec(memory_space=pl.ANY)
NT = (((1,), (1,)), ((), ()))
TN = (((0,), (0,)), ((), ()))


def stack_kernel(count, *refs):
    for k in range(count):
        refs[-1][k] = refs[k][...]


def stacked(blocks, behind):
    return pl.pallas_call(
        functools.partial(stack_kernel, len(blocks)),
        in_specs=[IN_VMEM] * len(blocks) + [IN_ANY] * len(behind),
        out_specs=IN_VMEM,
        out_shape=jax.ShapeDtypeStruct((len(blocks),) + blocks[0].shape, blocks[0].dtype),
        compiler_params=params(2),
        name="stacked",
    )(*blocks, *behind)


def hidden_kernel(n_row, n_col, kept, early, offsets, mine, theirs, weight, *refs):
    grad_out, token, *parts, grad_all, left = refs[-4 - len(kept) - len(early) :]
    token[...] = jnp.zeros_like(token)
    rows, part = mine.shape[1], parts[0].shape[0]
    kinds = [(p, F32) for p in kept] + [(p, BF16) for p in early]
    for x in range(n_row):
        grad_all[pl.ds(pl.multiple_of(offsets[x], rows), rows), :] = (theirs if x % 2 else mine)[x // 2]
    copy = pltpu.make_async_copy(grad_all, grad_out, left)
    step = stripe(weight.shape[0])
    for i in range(weight.shape[0] // step):
        at = slice(i * step, (i + 1) * step)
        total = lax.dot_general(grad_all[...], weight[at, :], NT, preferred_element_type=F32)
        if i == 0:
            copy.start()
        for ref, (p, kind) in zip(parts, kinds):
            ref[:, at] = total[p * part : (p + 1) * part].astype(kind)
    copy.wait()


def partial_hidden(mine, theirs, weight, behind, offsets, n_col, kept, early):
    n_row, rows, width = 2 * mine.shape[0], mine.shape[1], mine.shape[2]
    units = weight.shape[0]
    tokens = rows * n_row
    part = tokens // n_col
    grad_all, token, *parts = pl.pallas_call(
        functools.partial(hidden_kernel, n_row, n_col, kept, early),
        in_specs=[IN_SMEM] + [IN_VMEM] * 3 + [IN_HBM] * len(behind),
        out_specs=[IN_HBM] + [IN_VMEM] * (1 + len(kept) + len(early)),
        out_shape=[pltpu.HBM((tokens, width), BF16), jax.ShapeDtypeStruct((8, 128), F32)]
        + [jax.ShapeDtypeStruct((part, units), F32)] * len(kept)
        + [jax.ShapeDtypeStruct((part, units), BF16)] * len(early),
        scratch_shapes=[pltpu.VMEM((tokens, width), BF16), pltpu.SemaphoreType.DMA(())],
        compiler_params=params(3),
        cost_estimate=pl.CostEstimate(
            flops=2 * tokens * width * units, bytes_accessed=2 * units * width, transcendentals=0
        ),
        name="partial_hidden",
    )(offsets, mine, theirs, weight, *pinned(*behind))
    return grad_all, token, dict(zip(kept, parts)), dict(zip(early, parts[len(kept) :]))


def sum_kernel(count, *refs):
    total = refs[0][...]
    for ref in refs[1:count]:
        total = total + ref[...].astype(F32)
    refs[-1][...] = total.astype(BF16)


def summed(own, arrived, behind):
    return pl.pallas_call(
        functools.partial(sum_kernel, 1 + len(arrived)),
        in_specs=[IN_VMEM] * (1 + len(arrived)) + [IN_ANY] * len(behind),
        out_specs=IN_VMEM,
        out_shape=jax.ShapeDtypeStruct(own.shape, BF16),
        compiler_params=params(2),
        cost_estimate=pl.CostEstimate(flops=own.size, bytes_accessed=8 * own.size, transcendentals=0),
        name="summed",
    )(own, *arrived, *behind)


def pick(from_low, from_high, p, col, which, at):
    n_col = len(from_low)
    value, known = from_low[0][which, :, at], set()
    for c in range(n_col):
        below, distance = (c ^ p) < c, abs((c ^ p) - c)
        if p and (below, distance) not in known:
            known.add((below, distance))
            block = (from_low if below else from_high)[distance][which, :, at]
            match = jnp.logical_and(((col ^ p) < col) == below, jnp.abs((col ^ p) - col) == distance)
            value = block if len(known) == 1 else jnp.where(match, block, value)
    return value.astype(F32)


def down_kernel(n_col, scale, place, *refs):
    moved, grad_out = refs[: 2 * n_col - 1], refs[2 * n_col - 1]
    down_grad, up_factor, gate_factor, saved, grad_all, arrived, buffer, left = refs[-8:]
    loads = [pltpu.make_async_copy(block, saved.at[k], arrived.at[k]) for k, block in enumerate(moved)]
    loads.append(pltpu.make_async_copy(grad_out, grad_all, arrived.at[len(moved)]))
    for copy in loads:
        copy.start()
    waiting = set(range(len(moved)))
    blocks = [saved.at[k] for k in range(len(moved))]
    from_low, from_high = blocks[:n_col], blocks[:1] + blocks[n_col:]
    _, part, units = from_low[0].shape
    col = place[0]
    step = units // left.shape[0]
    copies = []
    for i in range(left.shape[0]):
        at = slice(i * step, (i + 1) * step)
        hidden = []
        for p in range(n_col):
            hops = {abs((c ^ p) - c) for c in range(n_col)}
            for k in sorted(waiting):
                if (k if k < n_col else k - n_col + 1) in hops:
                    loads[k].wait()
                    waiting.remove(k)
            g, u = (pick(from_low, from_high, p, col, which, at) for which in range(2))
            s = 1.0 / (1.0 + jnp.exp(-g))
            silu = g * s
            hidden.append((silu * u).astype(BF16))
            up_factor[p * part : (p + 1) * part, at] = silu
            gate_factor[p * part : (p + 1) * part, at] = u * s * (1.0 + g * (1.0 - s))
        if i == 0:
            loads[-1].wait()
        product = lax.dot_general(
            jnp.concatenate(hidden, axis=0), grad_all[...], TN, preferred_element_type=F32
        )
        buffer[at, :] = (product * scale).astype(BF16)
        copies.append(store(buffer, down_grad, left, i))
    for copy in copies:
        copy.wait()


def down_gradient(from_low, from_high, grad_all, behind, place, scale):
    n_col = len(from_low)
    units = from_low[0].shape[2]
    tokens, width = grad_all.shape
    return pl.pallas_call(
        functools.partial(down_kernel, n_col, scale),
        in_specs=[IN_SMEM] + [IN_ANY] * (2 * n_col - 1) + [IN_HBM] + [IN_ANY] * len(behind),
        out_specs=[IN_HBM] + [IN_VMEM] * 2,
        out_shape=[jax.ShapeDtypeStruct((units, width), BF16)] + [jax.ShapeDtypeStruct((tokens, units), F32)] * 2,
        scratch_shapes=[
            pltpu.VMEM((2 * n_col - 1,) + from_low[0].shape, BF16),
            pltpu.VMEM((tokens, width), BF16),
            pltpu.SemaphoreType.DMA((2 * n_col,)),
            pltpu.VMEM((units, width), BF16),
            pltpu.SemaphoreType.DMA((units // stripe(units),)),
        ],
        compiler_params=params(15),
        cost_estimate=pl.CostEstimate(
            flops=1 * 2 * tokens * width * units,
            bytes_accessed=2 * units * width + 12 * tokens * units,
            transcendentals=tokens * units,
        ),
        name="down_gradient",
    )(
        place, *pinned(*from_low[:-1]), from_low[-1], *pinned(*from_high[1:-1]), from_high[-1], *pinned(grad_all), *behind
    )


def input_kernel(n_row, n_col, offsets, *refs):
    hidden_grad, refs = refs[:n_col], refs[n_col:]
    up_factor, gate_factor, gate_weight, up_weight, _, gate_term, up_term, own, other, token = refs
    token[...] = jnp.zeros_like(token)
    part = hidden_grad[0].shape[0]
    rows = part * n_col // n_row
    half = own.shape[0]
    for j in range(n_col):
        h = hidden_grad[j][...].astype(F32)
        at = slice(j * part, (j + 1) * part)
        terms = ((gate_term, (h * gate_factor[at, :]).astype(BF16)), (up_term, (h * up_factor[at, :]).astype(BF16)))
        for c in range(part // rows):
            to = pl.ds(pl.multiple_of(offsets[j * (part // rows) + c], rows), rows)
            for ref, term in terms:
                ref[to, :] = term[c * rows : (c + 1) * rows]
    step = stripe(own.shape[1])
    for i in range(own.shape[1] // step):
        at = slice(i * step, (i + 1) * step)
        total = lax.dot_general(gate_term[...], gate_weight[at, :], NT, preferred_element_type=F32)
        total += lax.dot_general(up_term[...], up_weight[at, :], NT, preferred_element_type=F32)
        own[:, at] = total[:half]
        other[:, at] = total[half:]


def partial_input(hidden_grad, up_factor, gate_factor, gate_weight, up_weight, behind, offsets, n_row):
    n_col = len(hidden_grad)
    part, units = hidden_grad[0].shape
    tokens = part * n_col
    width = gate_weight.shape[0]
    return pl.pallas_call(
        functools.partial(input_kernel, n_row, n_col),
        in_specs=[IN_SMEM] + [IN_VMEM] * (n_col + 4) + [IN_ANY],
        out_specs=[IN_VMEM] * 5,
        out_shape=[jax.ShapeDtypeStruct((tokens, units), BF16)] * 2
        + [jax.ShapeDtypeStruct((tokens // 2, width), F32)] * 2
        + [jax.ShapeDtypeStruct((8, 128), F32)],
        compiler_params=params(2),
        cost_estimate=pl.CostEstimate(
            flops=4 * tokens * width * units, bytes_accessed=4 * units * width, transcendentals=0
        ),
        name="partial_input",
    )(offsets, *hidden_grad, up_factor, gate_factor, gate_weight, up_weight, behind)


def weight_kernel(scale, mine, theirs, gate_term, up_term, _, gate_grad, up_grad, buffers, left):
    blocks = mine.shape[0]
    step = buffers.shape[1] // left.shape[1]
    copies = []
    for i in range(left.shape[1]):
        at = slice(i * step, (i + 1) * step)
        left_side = jnp.concatenate([ref[k, :, at] for ref in (mine, theirs) for k in range(blocks)], axis=0)
        for k, (term, out) in enumerate(((gate_term, gate_grad), (up_term, up_grad))):
            product = lax.dot_general(left_side, term[...], TN, preferred_element_type=F32)
            buffers[k, at, :] = (product * scale).astype(BF16)
            copies.append(store(buffers.at[k], out, left.at[k], i))
    for copy in copies:
        copy.wait()


def weight_gradients(mine, theirs, gate_term, up_term, behind, scale):
    width = mine.shape[2]
    tokens, units = gate_term.shape
    return pl.pallas_call(
        functools.partial(weight_kernel, scale),
        in_specs=[IN_VMEM] * 4 + [IN_ANY],
        out_specs=[IN_HBM] * 2,
        out_shape=[jax.ShapeDtypeStruct((width, units), BF16)] * 2,
        scratch_shapes=[
            pltpu.VMEM((2, width, units), BF16),
            pltpu.SemaphoreType.DMA((2, width // stripe(width))),
        ],
        compiler_params=params(18),
        cost_estimate=pl.CostEstimate(
            flops=4 * tokens * width * units, bytes_accessed=4 * units * width, transcendentals=0
        ),
        name="weight_gradients",
    )(mine, theirs, gate_term, up_term, behind)


def per_device(inputs, grad_out, gate_pre, up_pre, gate_weight, up_weight, down_weight):
    n_row, n_col = lax.axis_size("row"), lax.axis_size("col")
    row, col = lax.axis_index("row"), lax.axis_index("col")
    rows = grad_out.shape[0]
    tokens = rows * n_row
    share = n_row // n_col
    scale = 1.0 / math.sqrt(tokens)

    block = row ^ jnp.arange(n_row, dtype=jnp.int32)
    to_parts = (((block // share) ^ col) * share + block % share) * rows
    part = col ^ jnp.arange(n_col, dtype=jnp.int32)
    seen = (part[:, None] * share + jnp.arange(share, dtype=jnp.int32)).reshape(-1) ^ row
    to_blocks = ((seen % 2) * (n_row // 2) + seen // 2) * rows

    near = [swap(grad_out, "row", mask) for mask in range(2, n_row, 2)]
    saved = jnp.stack([gate_pre, up_pre])
    low, high = relay_col(saved, saved, n_col, 1)
    from_low, from_high = [saved, low], [saved, high]
    grad_mine = stacked([grad_out] + near, [])
    fetched, _ = fetch([down_weight], [grad_mine])
    grad_theirs = swap(grad_mine, "row", 1)
    kept, early = ((0, 1, 3), (2, 3)) if n_col == 4 else (tuple(range(0, n_col, 2)), tuple(range(1, n_col, 2)))
    grad_all, token, parts, sends = partial_hidden(
        grad_mine, grad_theirs, fetched, [from_low[1], from_high[1]], to_parts.astype(jnp.int32), n_col, kept, early
    )

    (low, high), token = after((low, high), token)
    for step in range(2, n_col):
        low, high = relay_col(low, high, n_col, step)
        from_low.append(low)
        from_high.append(high)
    if n_col == 4:
        arrived, onward = reduce_line(parts, sends, col)
    else:
        arrived, onward = reduce_halves(parts, sends, n_col)
    (inputs, onward), token = after((inputs, onward[:8, :128]), token)
    input_mine = spread_row(inputs, n_row)
    own = summed(parts[0], arrived, [token, onward])
    gate_fetched, up_fetched, token = fetch([gate_weight, up_weight], [own])
    hidden_grad = spread_col(own, token, n_col)

    down_grad, up_factor, gate_factor = down_gradient(
        from_low, from_high, grad_all, [hidden_grad[n_col // 2]], col[None].astype(jnp.int32), scale
    )
    gate_term, up_term, mine, other, token = partial_input(
        hidden_grad, up_factor, gate_factor, gate_fetched, up_fetched, input_mine, to_blocks.astype(jnp.int32), n_row
    )

    mine = mine + swap(other, "row", 1)
    input_grad = mine[:rows]
    for k in range(1, n_row // 2):
        away = mine[k * rows : (k + 1) * rows].astype(BF16)
        input_grad = input_grad + swap(away, "row", 2 * k).astype(F32)
    input_mine, token = after(input_mine, token)
    input_theirs = swap(input_mine, "row", 1)
    gate_grad, up_grad = weight_gradients(input_mine, input_theirs, gate_term, up_term, token, scale)
    return (input_grad.astype(BF16), gate_grad, up_grad, down_grad)


def solution(mesh):
    return jax.shard_map(
        per_device,
        mesh=mesh,
        in_specs=(
            P("row", "col"),
            P("row", "col"),
            P("col", "row"),
            P("col", "row"),
            P("col", "row"),
            P("col", "row"),
            P("row", "col"),
        ),
        out_specs=(P("row", "col"), P("col", "row"), P("col", "row"), P("row", "col")),
        check_vma=False,
    )
```
